32 devices in a mesh: dp: 32 (over z, y, x, core).
Axes of the slice: x: 2, y: 2, z: 4, core: 2. Of those that a mesh axis runs over, the one named last changes fastest.
Arguments:
- tokens: bfloat16 [32, 1024, 512], P('dp'), may hold values from -6 to 6
- memory: bfloat16 [32, 1024, 512], P('dp'), may hold values from -6 to 6
- cotangent: bfloat16 [32, 1024, 512], P('dp'), may hold values from -6 to 6
- dec_segments: int32 [32, 1024], P('dp'), may hold values from -1 to 15, as said below
- mem_segments: int32 [32, 1024], P('dp'), may hold values from -1 to 15, as said below
- time_steps: int32 [32, 16], P('dp'), may hold values from 0 to 49
- time_table: bfloat16 [512, 50], P('dp'), may hold values from -3 to 3
- first_gain: bfloat16 [512], P('dp'), may hold values from 0.25 to 1.75
- first_bias: bfloat16 [512], P('dp'), may hold values from -2 to 2
- self_query: bfloat16 [512, 512], P('dp'), may hold values from -0.25 to 0.25
- self_key: bfloat16 [512, 512], P('dp'), may hold values from -0.25 to 0.25
- self_value: bfloat16 [512, 512], P('dp'), may hold values from -0.25 to 0.25
- self_out: bfloat16 [512, 512], P('dp'), may hold values from -1.5 to 1.5
- cross_query: bfloat16 [512, 512], P('dp'), may hold values from -0.25 to 0.25
- cross_key: bfloat16 [512, 512], P('dp'), may hold values from -0.25 to 0.25
- cross_value: bfloat16 [512, 512], P('dp'), may hold values from -0.25 to 0.25
- cross_out: bfloat16 [512, 512], P('dp'), may hold values from -1.5 to 1.5
- second_gain: bfloat16 [512], P('dp'), may hold values from 0.25 to 1.75
- second_bias: bfloat16 [512], P('dp'), may hold values from -2 to 2
- expand_weight: bfloat16 [512, 2048], P('dp'), may hold values from -0.25 to 0.25
- expand_bias: bfloat16 [2048], P('dp'), may hold values from -3 to 3
- shrink_weight: bfloat16 [2048, 512], P('dp'), may hold values from -0.25 to 0.25
- shrink_bias: bfloat16 [512], P('dp'), may hold values from -2 to 2
Outputs:
- layer_out: bfloat16 [32, 1024, 512], P('dp')
- tokens_grad: float32 [32, 1024, 512], P('dp')
- memory_grad: float32 [32, 1024, 512], P('dp')
- time_table_grad: float32 [512, 50], P('dp')
- first_gain_grad: float32 [512], P('dp')
- first_bias_grad: float32 [512], P('dp')
- self_query_grad: float32 [512, 512], P('dp')
- self_key_grad: float32 [512, 512], P('dp')
- self_value_grad: float32 [512, 512], P('dp')
- self_out_grad: float32 [512, 512], P('dp')
- cross_query_grad: float32 [512, 512], P('dp')
- cross_key_grad: float32 [512, 512], P('dp')
- cross_value_grad: float32 [512, 512], P('dp')
- cross_out_grad: float32 [512, 512], P('dp')
- second_gain_grad: float32 [512], P('dp')
- second_bias_grad: float32 [512], P('dp')
- expand_weight_grad: float32 [512, 2048], P('dp')
- expand_bias_grad: float32 [2048], P('dp')
- shrink_weight_grad: float32 [2048, 512], P('dp')
- shrink_bias_grad: float32 [512], P('dp')
The draws below stay inside these ranges and needn't reach their ends.
Inputs may be any that keep to these rules, and one draw needn't show every extreme that they name: `dec_segments`: in each row the ids are 0 to 15, never falling, each present, over a prefix of the row; the remaining slots (at least one) hold -1. `mem_segments`: in each row the ids are 0 to 15, never falling, each present, over a prefix of the row; the remaining slots (at least one) hold -1.
All inputs are finite; a program needn't handle non-finite values.
Results may differ from the reference program's by a relative error of at most 0.03.
The reference program's roundings to bfloat16 on the way count: a program that leaves them out, or rounds other values in their place, can miss the bound.
Values may be sent and summed in bfloat16 or wider, within the bound.
A program may use at most 192 MiB of HBM per device.

```python
import jax
import jax.numpy as jnp
from jax import lax

D = 512
HEADS = 8
HEAD_DIM = 64
FF = 2048
TSTEPS = 50
NSEG = 16
LEN = 1024
MLEN = 1024
ROWS = 32


def segment_ids(key, length):
    fill_key, offset_key = jax.random.split(key)
    fill_len = jax.random.randint(fill_key, (ROWS, 1), length // 2, length)
    spread_len = fill_len // (4 * NSEG)
    base_bounds = jnp.arange(1, NSEG, dtype=jnp.int32)[None, :] * fill_len // NSEG
    offsets = jax.random.randint(offset_key, (ROWS, NSEG - 1), -spread_len, spread_len + 1)
    bounds = base_bounds + offsets
    positions = jnp.arange(length, dtype=jnp.int32)[None, :]
    seg_ids = jnp.sum((positions[:, :, None] >= bounds[:, None, :]).astype(jnp.int32), axis=-1)
    return jnp.where(positions < fill_len, seg_ids, -1).astype(jnp.int32)


def draw_dec_segments(key, part):
    key = jax.random.fold_in(key, 11)
    return segment_ids(key, LEN)


def draw_mem_segments(key, part):
    key = jax.random.fold_in(key, 23)
    return segment_ids(key, MLEN)


def place_ends(values, key, smallest, top_value):
    place = [jax.random.randint(jax.random.fold_in(key, axis), (), 0, length) for axis, length in enumerate(values.shape)]
    widest = values.shape.index(max(values.shape))
    beside = place[:widest] + [(place[widest] + 1) % values.shape[widest]] + place[widest + 1:]
    return values.at[tuple(place)].set(smallest).at[tuple(beside)].set(top_value)


def level_of(stream_key, extent, shards, low, top_value):
    loudness = 1.0
    for dim, parts in shards:
        steps = jax.random.uniform(jax.random.fold_in(jax.random.fold_in(stream_key, 6), dim), (parts,), jnp.float32, low / len(shards), top_value / len(shards))
        loudness = loudness * jnp.repeat(jnp.exp(steps), extent[dim] // parts).reshape((-1,) + (1,) * (len(extent) - 1 - dim))
    return loudness


def bell_draw(stream_key, dims, deviation, limit, shards=(), kind=jnp.bfloat16):
    factor_of = level_of(stream_key, dims, shards, -0.22, 0.18) if shards else 1.0
    values = jax.random.normal(stream_key, dims, jnp.float32) * deviation * factor_of
    return jnp.minimum(jnp.maximum(values, -limit), limit).astype(kind)


def setup_inputs(seed: int = 0) -> dict:
    seeds = jax.random.split(jax.random.key(seed), 24)
    tokens = bell_draw(seeds[0], (ROWS, LEN, D), 1.0, 6.0, ((0, 32),))
    memory = bell_draw(seeds[1], (ROWS, MLEN, D), 1.0, 6.0, ((0, 32),))
    cotangent = bell_draw(seeds[2], (ROWS, LEN, D), 1.0, 6.0, ((0, 32),))
    dec_segments = draw_dec_segments(jax.random.fold_in(seeds[23], 71), 0)
    mem_segments = draw_mem_segments(jax.random.fold_in(seeds[23], 71), 0)
    time_steps = place_ends(jax.random.randint(seeds[5], (ROWS, NSEG), 0, TSTEPS), jax.random.fold_in(seeds[5], 1), 0, TSTEPS - 1).astype(jnp.int32)
    time_table = bell_draw(seeds[6], (D, TSTEPS), 0.5, 3.0, ((0, 32),))
    first_gain = jnp.clip(1.0 + 0.15 * jax.random.normal(seeds[7], (D,), jnp.float32), 0.25, 1.75).astype(jnp.bfloat16)
    first_bias = bell_draw(seeds[8], (D,), 0.3, 2.0, ((0, 32),))
    self_query = bell_draw(seeds[9], (D, D), D ** -0.5, 0.25, ((0, 32),))
    self_key = bell_draw(seeds[10], (D, D), D ** -0.5, 0.25, ((0, 32),))
    self_value = bell_draw(seeds[11], (D, D), D ** -0.5, 0.25, ((0, 32),))
    self_out = bell_draw(seeds[12], (D, D), (D // 32) ** -0.5, 1.5, ((0, 32),))
    cross_query = bell_draw(seeds[13], (D, D), D ** -0.5, 0.25, ((0, 32),))
    cross_key = bell_draw(seeds[14], (D, D), D ** -0.5, 0.25, ((0, 32),))
    cross_value = bell_draw(seeds[15], (D, D), D ** -0.5, 0.25, ((0, 32),))
    cross_out = bell_draw(seeds[16], (D, D), (D // 32) ** -0.5, 1.5, ((0, 32),))
    second_gain = jnp.clip(1.0 + 0.15 * jax.random.normal(seeds[17], (D,), jnp.float32), 0.25, 1.75).astype(jnp.bfloat16)
    second_bias = bell_draw(seeds[18], (D,), 0.3, 2.0, ((0, 32),))
    expand_weight = bell_draw(seeds[19], (D, FF), D ** -0.5, 0.25, ((0, 32),))
    expand_bias = bell_draw(seeds[20], (FF,), 0.5, 3.0, ((0, 32),))
    shrink_weight = bell_draw(seeds[21], (FF, D), (FF // 4) ** -0.5, 0.25, ((0, 32),))
    shrink_bias = bell_draw(seeds[22], (D,), 0.3, 2.0, ((0, 32),))
    return {"tokens": tokens, "memory": memory, "cotangent": cotangent, "dec_segments": dec_segments, "mem_segments": mem_segments, "time_steps": time_steps, "time_table": time_table, "first_gain": first_gain, "first_bias": first_bias, "self_query": self_query, "self_key": self_key, "self_value": self_value, "self_out": self_out, "cross_query": cross_query, "cross_key": cross_key, "cross_value": cross_value, "cross_out": cross_out, "second_gain": second_gain, "second_bias": second_bias, "expand_weight": expand_weight, "expand_bias": expand_bias, "shrink_weight": shrink_weight, "shrink_bias": shrink_bias}


EPS = 1e-05
NEG = -1e+30
HIGH = lax.Precision.HIGHEST

@jax.custom_vjp
def low(v):
    return lax.optimization_barrier(v.astype(jnp.bfloat16)).astype(jnp.float32)

@jax.custom_vjp
def low_back(v):
    return v

def low_keep(v):
    return (low(v), None)

def low_pass(kept, grad):
    return (grad,)

def back_keep(v):
    return (v, None)

def back_low(kept, grad):
    return (low(grad),)
low.defvjp(low_keep, low_pass)
low_back.defvjp(back_keep, back_low)

def both_ways(values):
    return low(low_back(values))

def layer_norm(values, gain, offset):
    centre_mean = lax.optimization_barrier(jnp.mean(values, axis=-1, keepdims=True))
    centred = values - centre_mean
    spread_var = lax.optimization_barrier(jnp.mean(centred * centred, axis=-1, keepdims=True))
    return centred * lax.rsqrt(spread_var + EPS) * gain + offset

def matmul(left, right):
    return jnp.dot(left, right, precision=HIGH)

def attend(query_rows, key_rows, value_rows, seg_query, seg_keys):
    length = query_rows.shape[0]
    model_width = query_rows.shape[1]
    block_rows = min(512, length)
    q_blocks = query_rows.reshape(length // block_rows, block_rows, HEADS, HEAD_DIM)
    s_blocks = seg_query.reshape(length // block_rows, block_rows)
    key_heads = key_rows.reshape(key_rows.shape[0], HEADS, HEAD_DIM)
    value_heads = value_rows.reshape(value_rows.shape[0], HEADS, HEAD_DIM)

    def one_block(paired):
        q_part, s_part = paired
        scores = low_back(jnp.einsum('qhd,khd->hqk', q_part, key_heads, precision=HIGH))
        allowed = (s_part[:, None] == seg_keys[None, :])[None]
        scores = jnp.where(allowed, scores, NEG)
        row_max = lax.optimization_barrier(jnp.max(scores, axis=-1, keepdims=True))
        expo_vals = jnp.exp(scores - row_max)
        soft_weights = low(expo_vals / lax.optimization_barrier(jnp.sum(expo_vals, axis=-1, keepdims=True)))
        mixed_part = jnp.einsum('hqk,khd->qhd', soft_weights, value_heads, precision=HIGH)
        return mixed_part.reshape(block_rows, model_width)
    return lax.map(jax.checkpoint(one_block), (q_blocks, s_blocks)).reshape(length, model_width)

def slot_table(seg_row, steps_row):
    seg_picks = (seg_row[:, None] == jnp.arange(NSEG, dtype=jnp.int32)[None, :]).astype(jnp.float32)
    step_picks = (steps_row[:, None] == jnp.arange(TSTEPS, dtype=jnp.int32)[None, :]).astype(jnp.float32)
    return matmul(seg_picks, step_picks)

def layer_row(input_rows, memory_rows, params, seg_dec, seg_mem, slot_steps):
    time_rows, gain_one, bias_one, w_query, w_key, w_value, w_out, c_query, c_key, c_value, c_out, gain_two, bias_two, w_expand, b_expand, w_shrink, b_shrink = params
    scaling = HEAD_DIM ** (-0.5)
    start_rows = input_rows + matmul(slot_steps, time_rows.T)
    normed_one = low(layer_norm(start_rows, gain_one, bias_one))
    query_rows = low(low_back(matmul(normed_one, w_query)) * scaling)
    key_rows = both_ways(matmul(normed_one, w_key))
    value_rows = both_ways(matmul(normed_one, w_value))
    self_mixed = both_ways(attend(query_rows, key_rows, value_rows, seg_dec, seg_dec))
    after_self = start_rows + low_back(matmul(self_mixed, w_out))
    after_low = low(after_self)
    cross_q = low(low_back(matmul(after_low, c_query)) * scaling)
    cross_k = both_ways(matmul(memory_rows, c_key))
    cross_v = both_ways(matmul(memory_rows, c_value))
    cross_mixed = both_ways(attend(cross_q, cross_k, cross_v, seg_dec, seg_mem))
    after_cross = after_self + low_back(matmul(cross_mixed, c_out))
    normed_two = low(layer_norm(after_cross, gain_two, bias_two))
    pre_act = low_back(matmul(normed_two, w_expand) + b_expand)
    act_low = low(jax.nn.gelu(pre_act, approximate=False))
    branch = low_back(matmul(act_low, w_shrink) + b_shrink)
    keep_rows = (seg_dec >= 0).astype(jnp.float32)[:, None]
    return keep_rows * (after_cross + branch)

def reference(tokens, memory, cotangent, dec_segments, mem_segments, time_steps, time_table, first_gain, first_bias, self_query, self_key, self_value, self_out, cross_query, cross_key, cross_value, cross_out, second_gain, second_bias, expand_weight, expand_bias, shrink_weight, shrink_bias):
    params = tuple((item.astype(jnp.float32) for item in (time_table, first_gain, first_bias, self_query, self_key, self_value, self_out, cross_query, cross_key, cross_value, cross_out, second_gain, second_bias, expand_weight, expand_bias, shrink_weight, shrink_bias)))
    zero_grads = tuple((jnp.zeros_like(item) for item in params))

    def per_row(totals, row_items):
        input_row, memory_row, cot_row, seg_dec, seg_mem, steps_row = row_items
        slot_steps = slot_table(seg_dec, steps_row)

        def forward(input_rows, memory_rows, weights):
            return layer_row(input_rows, memory_rows, weights, seg_dec, seg_mem, slot_steps)
        output_row, pull_back = jax.vjp(forward, input_row.astype(jnp.float32), memory_row.astype(jnp.float32), params)
        grad_input, grad_memory, grad_params = pull_back(cot_row.astype(jnp.float32))
        totals = jax.tree.map(jnp.add, totals, grad_params)
        return (totals, (output_row.astype(jnp.bfloat16), grad_input, grad_memory))
    totals, (outputs, input_grads, memory_grads) = lax.scan(per_row, zero_grads, (tokens, memory, cotangent, dec_segments, mem_segments, time_steps))
    return (outputs, input_grads, memory_grads, totals[0], totals[1], totals[2], totals[3], totals[4], totals[5], totals[6], totals[7], totals[8], totals[9], totals[10], totals[11], totals[12], totals[13], totals[14], totals[15], totals[16])
```

```python
import functools

import jax
import jax.numpy as jnp
from jax import lax
from jax.experimental import pallas as pl
from jax.experimental.pallas import tpu as pltpu
from jax.sharding import PartitionSpec as P

HEADS = 8
EPS = 1e-05
NEG = -1e30
F32 = jnp.float32
BF16 = jnp.bfloat16
MESH = pl.DeviceIdType.MESH
TILE = 128
VMEM_BYTES = 60 * 1024 * 1024
ROW_TILE = 256


def vmem_spec():
    return pl.BlockSpec(memory_space=pltpu.VMEM)


def smem_spec():
    return pl.BlockSpec(memory_space=pltpu.SMEM)


def hbm_spec():
    return pl.BlockSpec(memory_space=pl.ANY)


def dot(a, b):
    return lax.dot_general(a, b, (((1,), (0,)), ((), ())), preferred_element_type=F32)


def dot_nt(a, b):
    return lax.dot_general(a, b, (((1,), (1,)), ((), ())), preferred_element_type=F32)


def bit_index(bits, free, fixed):
    return tuple(slice(None) if b in free else fixed[b] for b in range(bits - 1, -1, -1))


def link_orders(bits):
    link = list(range(bits - 1, 0, -1))
    if len(link) != 4:
        return [(link, 1)]
    return [([4, 3, 2, 1], 5), ([4, 3, 1, 2], 5), ([1, 2, 4, 3], 3)]


def enter(bits, me):
    barrier = pltpu.get_barrier_semaphore()
    for b in range(bits):
        pl.semaphore_signal(barrier, inc=1, device_id=(me ^ (1 << b),), device_id_type=MESH)
    pl.semaphore_wait(barrier, bits)


def gather_kernel(bits, parts, *refs):
    ins, (one, two), (local_sem, send_sem, recv_sem) = refs[:11], refs[11:13], refs[13:]
    me = lax.axis_index("dp")
    mine = {b: lax.rem(me // (1 << b), 2) for b in range(bits)}
    own = bit_index(bits, (), mine)
    local = []
    for j in range(8):
        local.append((ins[j], one.at[(j,) + own]))
    for j in range(4):
        local.append((ins[8].at[:, pl.ds(512 * j, 512)], one.at[(8 + j,) + own]))
    local.append((ins[9], one.at[(12,) + own]))
    local.append((ins[10], two.at[own]))
    copies = [
        pltpu.make_async_copy(src, dst, local_sem.at[i]) for i, (src, dst) in enumerate(local)
    ]
    for c in copies:
        c.start()
    enter(bits, me)
    for c in copies:
        c.wait()
    bufs = (one, two)
    count = [0]
    pending = []

    def send(view, target):
        i = count[0]
        count[0] += 1
        c = pltpu.make_async_remote_copy(
            src_ref=view,
            dst_ref=view,
            send_sem=send_sem.at[i],
            recv_sem=recv_sem.at[i],
            device_id=(target,),
            device_id_type=MESH,
        )
        c.start()
        return c

    def view_of(part, free, fixed):
        which, blocks, _ = part
        index = bit_index(bits, free, fixed)
        if which == 0:
            return bufs[0].at[(slice(blocks[0], blocks[1]),) + index]
        return bufs[1].at[index + (slice(blocks[0], blocks[1]),)]

    current = []
    for part in parts:
        order = part[2]
        current.append(send(view_of(part, (), mine), me ^ (1 << order[0])))
        pending.append(send(view_of(part, (), mine), me ^ 1))
    steps = bits - 1
    for s in range(steps):
        for p, part in enumerate(parts):
            order = part[2]
            current[p].wait_recv()
            pending.append((current[p],))
            if s + 1 < steps:
                current[p] = send(
                    view_of(part, tuple(order[: s + 1]), mine), me ^ (1 << order[s + 1])
                )
            other = dict(mine)
            other[order[s]] = 1 - mine[order[s]]
            pending.append(send(view_of(part, tuple(order[:s]), other), me ^ 1))
    for c in pending:
        if isinstance(c, tuple):
            c[0].wait_send()
        else:
            c.wait()


def gather_parts(bits):
    orders = link_orders(bits)
    if len(orders) == 1:
        return [(0, (0, 13), orders[0][0]), (1, (0, 64), orders[0][0])]
    a, b, c = (o for o, _ in orders)
    return [
        (0, (0, 5), a),
        (0, (5, 10), b),
        (0, (10, 13), c),
        (1, (0, 32), a),
        (1, (32, 64), b),
    ]


def gather_all(n, arrays):
    bits = n.bit_length() - 1
    two = (2,) * bits
    parts = gather_parts(bits)
    sends = len(parts) * (2 * (bits - 1) + 1)
    return pl.pallas_call(
        functools.partial(gather_kernel, bits, parts),
        out_shape=(
            jax.ShapeDtypeStruct((13,) + two + (16, 512), BF16),
            jax.ShapeDtypeStruct(two + (64, 512), BF16),
        ),
        in_specs=[vmem_spec()] * 11,
        out_specs=(hbm_spec(), hbm_spec()),
        scratch_shapes=[
            pltpu.SemaphoreType.DMA((14,)),
            pltpu.SemaphoreType.DMA((sends,)),
            pltpu.SemaphoreType.DMA((sends,)),
        ],
        compiler_params=pltpu.CompilerParams(collective_id=0, has_side_effects=True),
        name="gather_weights",
    )(*arrays)


def scatter_kernel(bits, parts, *refs):
    attn, expand, small, two, out = refs[:5]
    r_core, work, stage_refs = refs[5], refs[6], refs[7:-2]
    send_sem, recv_sem = refs[-2:]
    me = lax.axis_index("dp")
    mine = {b: lax.rem(me // (1 << b), 2) for b in range(bits)}
    links = bits - 1
    lead = (slice(None),) * links
    enter(bits, me)
    count = [0]

    def send(src, dst, target):
        i = count[0]
        count[0] += 1
        c = pltpu.make_async_remote_copy(
            src_ref=src,
            dst_ref=dst,
            send_sem=send_sem.at[i],
            recv_sem=recv_sem.at[i],
            device_id=(target,),
            device_id_type=MESH,
        )
        c.start()
        return c

    def link_index(free, fixed):
        return tuple(slice(None) if b in free else fixed[b] for b in range(links, 0, -1))

    def send_core(part):
        blocks, _ = part
        sent = []
        low, high = blocks
        for ref, first, end in ((attn, 0, 8), (expand, 8, 12), (small, 12, 13)):
            start, stop = max(low, first), min(high, end)
            if start < stop:
                src = ref.at[(slice(start - first, stop - first),) + lead + (1 - mine[0],)]
                sent.append(send(src, r_core.at[start:stop], me ^ 1))
        for j in range(max(low, 13), high):
            src = two.at[lead + (1 - mine[0], slice(16 * (j - 13), 16 * (j - 12)))]
            sent.append(send(src, r_core.at[j], me ^ 1))
        return sent

    def positions(free):
        where = [()]
        for b in range(links, 0, -1):
            where = [w + (v,) for w in where for v in ((0, 1) if b in free else (mine[b],))]
        return where


    def add_core(part):
        low, high = part[0]
        where = positions(tuple(range(1, bits)))

        def add(j, w, own):
            work[(j,) + w] = (own.astype(F32) + r_core[(j,) + w].astype(F32)).astype(BF16)

        for ref, first, end in ((attn, 0, 8), (expand, 8, 12), (small, 12, 13)):

            def block(j, carry):
                for w in where:
                    add(j, w, ref[(j - first,) + w + (mine[0],)])
                return carry

            lax.fori_loop(max(low, first), max(low, first, min(high, end)), block, 0)
        for j in range(max(low, 13), high):
            for w in where:
                add(j, w, two[w + (mine[0], slice(16 * (j - 13), 16 * (j - 12)))])

    def send_link(part, s):
        (low, high), order = part
        free = tuple(order[s + 1 :])
        other = dict(mine)
        other[order[s]] = 1 - mine[order[s]]
        src = work.at[(slice(low, high),) + link_index(free, other)]
        return send(src, stage_refs[s].at[low:high], me ^ (1 << order[s]))

    def add_link(part, s):
        (low, high), order = part
        free = tuple(order[s + 1 :])
        where = positions(free)
        inner = [()]
        for _ in free:
            inner = [w + (v,) for w in inner for v in (0, 1)]

        def block(j, carry):
            for w, r in zip(where, inner):
                work[(j,) + w] = (
                    work[(j,) + w].astype(F32) + stage_refs[s][(j,) + r].astype(F32)
                ).astype(BF16)
            return carry

        if s + 1 < links:
            lax.fori_loop(low, high, block, 0)
            return
        for j in range(low, high):
            w = where[0]
            total = work[(j,) + w].astype(F32) + stage_refs[s][j].astype(F32)
            out[j] = total

    started = []
    current = [send_core(part) for part in parts]
    for s in range(-1, links):
        for p, part in enumerate(parts):
            for c in current[p]:
                c.wait_recv()
            started.extend(current[p])
            if s < 0:
                add_core(part)
            else:
                add_link(part, s)
            if s + 1 < links:
                current[p] = [send_link(part, s + 1)]
    for c in started:
        c.wait_send()


def scatter_sums(n, attn, expand, small, shrink):
    bits = n.bit_length() - 1
    links = bits - 1
    orders = link_orders(bits)
    if len(orders) == 1:
        parts = [((0, 17), orders[0][0][::-1])]
    else:
        a, b, c = (o[::-1] for o, _ in orders)
        parts = [((0, 7), a), ((7, 13), b), ((13, 17), c)]
    sends = len(parts) * links + 7 + len(parts)
    halves = (2,) * links
    devices = (2,) * bits
    return pl.pallas_call(
        functools.partial(scatter_kernel, bits, parts),
        out_shape=jax.ShapeDtypeStruct((17, 16, 512), F32),
        in_specs=[vmem_spec()] * 4,
        out_specs=vmem_spec(),
        scratch_shapes=[
            pltpu.VMEM((17,) + halves + (16, 512), BF16),
            pltpu.VMEM((17,) + halves + (16, 512), BF16),
        ]
        + [pltpu.VMEM((17,) + halves[: links - 1 - s] + (16, 512), BF16) for s in range(links)]
        + [pltpu.SemaphoreType.DMA((sends,)), pltpu.SemaphoreType.DMA((sends,))],
        compiler_params=pltpu.CompilerParams(
            collective_id=1, has_side_effects=True, vmem_limit_bytes=VMEM_BYTES
        ),
        name="scatter_sums",
    )(
        attn.reshape((8,) + devices + (16, 512)),
        expand.reshape((4,) + devices + (16, 512)),
        small.reshape((1,) + devices + (16, 512)),
        shrink.reshape(devices + (64, 512)),
    )


def split_kernel(sums, *outs):
    for j in range(8):
        outs[j][...] = sums[j]
    for j in range(4):
        outs[8][:, 512 * j : 512 * (j + 1)] = sums[8 + j]
        outs[9][16 * j : 16 * (j + 1), :] = sums[13 + j]
    outs[10][...] = sums[12]


def split_sums(sums):
    shapes = [(16, 512)] * 8 + [(16, 2048), (64, 512), (16, 512)]
    return pl.pallas_call(
        split_kernel,
        out_shape=tuple(jax.ShapeDtypeStruct(shape, F32) for shape in shapes),
        in_specs=[vmem_spec()],
        out_specs=tuple([vmem_spec()] * 11),
        name="split_sums",
    )(sums)


def each_tile(length, size, body):
    def step(i, carry):
        body(pl.multiple_of(i * size, size))
        return carry

    lax.fori_loop(0, length // size, step, 0)


def transpose_into(target, source, dtype=BF16):
    def tile(r):
        target[:, pl.ds(r, TILE)] = source[pl.ds(r, TILE), :].T.astype(dtype)

    each_tile(source.shape[0], TILE, tile)


def fill_columns(target, row_ref):
    def tile(r):
        row = row_ref[:, pl.ds(r, TILE)].astype(F32)
        target[pl.ds(r, TILE), :] = jnp.broadcast_to(row, (TILE, TILE)).T

    each_tile(row_ref.shape[1], TILE, tile)


def normalise(x):
    centred = x - jnp.mean(x, axis=-1, keepdims=True)
    rstd = lax.rsqrt(jnp.mean(centred * centred, axis=-1, keepdims=True) + EPS)
    return centred * rstd, rstd


def norm_backward(grad, hat, rstd, gain):
    scaled = grad * gain
    first = jnp.mean(scaled, axis=-1, keepdims=True)
    second = jnp.mean(scaled * hat, axis=-1, keepdims=True)
    return rstd * (scaled - first - hat * second)


def even_rows(shape):
    return (lax.broadcasted_iota(jnp.int32, shape, 0) & 64) == 0


def even_lanes(shape):
    return (lax.broadcasted_iota(jnp.int32, shape, 1) & 64) == 0


def mask_rows(target, block):
    even = even_rows(block.shape)
    zero = jnp.zeros_like(block)
    target[:, :TILE] = jnp.where(even, block, zero)
    target[:, TILE:] = jnp.where(even, zero, block)


def mask_lanes(target, block):
    even = even_lanes(block.shape)
    zero = jnp.zeros_like(block)
    target[:TILE, :] = jnp.where(even, block, zero)
    target[TILE:, :] = jnp.where(even, zero, block)


def attend(k_ref, q_t, v_t, key_cols, query_row, bounds, which, out_t, lse, q_pair, acc):
    width = out_t.shape[0]
    pairs = width // TILE

    def query_block(q0):
        i = q0 // TILE
        here = pl.ds(q0, TILE)
        mask_rows(q_pair, q_t[:, here])
        seg_q = query_row[:, here].astype(F32)
        acc[...] = jnp.zeros_like(acc)

        def key_block(kb, carry):
            there = pl.ds(pl.multiple_of(kb * TILE, TILE), TILE)
            bias = jnp.where(key_cols[there, :] == seg_q, 0.0, NEG)
            bias = jnp.concatenate([bias, bias], axis=1)
            result = []
            for p in range(pairs):
                lanes = slice(TILE * p, TILE * (p + 1))
                top, total = carry[p]
                scores = dot(k_ref[there, lanes], q_pair[lanes, :]) + bias
                now = jnp.maximum(top, jnp.max(scores, axis=0, keepdims=True))
                expo = jnp.exp(scores - now)
                shrink = jnp.exp(top - now)
                total = total * shrink + jnp.sum(expo, axis=0, keepdims=True)
                low = expo.astype(BF16)
                for h in range(2):
                    rows = slice(TILE * p + 64 * h, TILE * p + 64 * (h + 1))
                    cols = slice(TILE * h, TILE * (h + 1))
                    acc[rows, :] = acc[rows, :] * shrink[:, cols] + dot(
                        v_t[rows, there], low[:, cols]
                    )
                result.append((now, total))
            return tuple(result)

        start = tuple(
            (jnp.full((1, 2 * TILE), NEG, F32), jnp.zeros((1, 2 * TILE), F32))
            for _ in range(pairs)
        )
        done = lax.fori_loop(bounds[which, i], bounds[which + 1, i], key_block, start)
        for p in range(pairs):
            top, total = done[p]
            inverse = 1.0 / total
            level = top + jnp.log(total)
            for h in range(2):
                rows = slice(TILE * p + 64 * h, TILE * p + 64 * (h + 1))
                cols = slice(TILE * h, TILE * (h + 1))
                out_t[rows, here] = (acc[rows, :] * inverse[:, cols]).astype(BF16)
                lse[2 * p + h : 2 * p + h + 1, here] = level[:, cols]

    each_tile(q_t.shape[1], TILE, query_block)


def attend_back(
    q_ref, k_ref, v_ref, g_ref, q_t, k_t, g_t, out_t, lse, key_cols, query_row, bounds, which,
    scale, dq_t, dk, dv, q_rows, g_rows, q_lanes, g_lanes, acc,
):
    width = out_t.shape[0]
    pairs = width // TILE

    def clear(r):
        dk[pl.ds(r, TILE), :] = jnp.zeros((TILE, width), F32)
        dv[pl.ds(r, TILE), :] = jnp.zeros((TILE, width), F32)

    each_tile(dk.shape[0], TILE, clear)

    def query_block(q0):
        i = q0 // TILE
        here = pl.ds(q0, TILE)
        mask_rows(q_rows, q_t[:, here])
        mask_rows(g_rows, g_t[:, here])
        mask_lanes(q_lanes, q_ref[here, :])
        mask_lanes(g_lanes, g_ref[here, :])
        seg_q = query_row[:, here].astype(F32)
        acc[...] = jnp.zeros_like(acc)
        centres, levels = [], []
        for p in range(pairs):
            both = []
            for h in range(2):
                rows = slice(TILE * p + 64 * h, TILE * p + 64 * (h + 1))
                both.append(
                    jnp.sum(
                        g_t[rows, here].astype(F32) * out_t[rows, here].astype(F32),
                        axis=0,
                        keepdims=True,
                    )
                )
            centres.append(jnp.concatenate(both, axis=1))
            levels.append(
                jnp.concatenate(
                    [lse[2 * p : 2 * p + 1, here], lse[2 * p + 1 : 2 * p + 2, here]], axis=1
                )
            )

        def key_block(kb, carry):
            there = pl.ds(pl.multiple_of(kb * TILE, TILE), TILE)
            bias = jnp.where(key_cols[there, :] == seg_q, 0.0, NEG)
            bias = jnp.concatenate([bias, bias], axis=1)
            for p in range(pairs):
                lanes = slice(TILE * p, TILE * (p + 1))
                scores = dot(k_ref[there, lanes], q_rows[lanes, :]) + bias
                probs = jnp.exp(scores - levels[p])
                grads = dot(v_ref[there, lanes], g_rows[lanes, :])
                low = (probs * (grads - centres[p])).astype(BF16)
                dv[there, lanes] = dv[there, lanes] + dot(probs.astype(BF16), g_lanes[:, lanes])
                dk[there, lanes] = dk[there, lanes] + dot(low, q_lanes[:, lanes])
                for h in range(2):
                    rows = slice(TILE * p + 64 * h, TILE * p + 64 * (h + 1))
                    cols = slice(TILE * h, TILE * (h + 1))
                    acc[rows, :] = acc[rows, :] + dot(k_t[rows, there], low[:, cols])
            return carry

        lax.fori_loop(bounds[which, i], bounds[which + 1, i], key_block, 0)
        dq_t[:, here] = (acc[...] * scale).astype(BF16)

    each_tile(q_t.shape[1], TILE, query_block)


def forward_kernel(
    scale, steps, bounds, tokens, memory, dec, mem, weights, small,
    start, q, k, v, after_low, cq, ck, cv, mixed_t, lse, cross_t, cross_lse, after_cross,
    small_t, table, dec_cols, mem_cols, q_t, v_t, q_pair, acc,
):
    length, width = tokens.shape
    small_t[...] = small[:, :TILE].astype(F32).T
    table[...] = jnp.zeros_like(table)
    for s in range(steps.shape[1]):
        table[s : s + 1, :] = small_t[pl.ds(steps[0, s], 1), :]
    fill_columns(dec_cols, dec)
    fill_columns(mem_cols, mem)
    gain, offset = small_t[64:65, :], small_t[65:66, :]

    def first(r):
        rows = pl.ds(r, ROW_TILE)
        ids = lax.broadcasted_iota(jnp.int32, (ROW_TILE, TILE), 1).astype(F32)
        picks = jnp.where(dec_cols[rows, :] == ids, 1.0, 0.0).astype(BF16)
        begin = tokens[rows, :].astype(F32) + dot(picks, table[...].astype(BF16))
        start[rows, :] = begin
        hat, _ = normalise(begin)
        normed = (hat * gain + offset).astype(BF16)
        query = (dot(normed, weights[0]) * scale).astype(BF16)
        q[rows, :] = query
        q_t[:, rows] = query.T
        k[rows, :] = dot(normed, weights[1]).astype(BF16)
        value = dot(normed, weights[2]).astype(BF16)
        v[rows, :] = value
        v_t[:, rows] = value.T

    each_tile(length, ROW_TILE, first)
    attend(k, q_t, v_t, dec_cols, dec, bounds, 0, mixed_t, lse, q_pair, acc)

    def second(r):
        rows = pl.ds(r, ROW_TILE)
        after = start[rows, :] + dot(mixed_t[:, rows].T, weights[3])
        after_cross[rows, :] = after
        low = after.astype(BF16)
        after_low[rows, :] = low
        query = (dot(low, weights[4]) * scale).astype(BF16)
        cq[rows, :] = query
        q_t[:, rows] = query.T

    each_tile(length, ROW_TILE, second)

    def third(r):
        rows = pl.ds(r, ROW_TILE)
        ck[rows, :] = dot(memory[rows, :], weights[5]).astype(BF16)
        value = dot(memory[rows, :], weights[6]).astype(BF16)
        cv[rows, :] = value
        v_t[:, rows] = value.T

    each_tile(memory.shape[0], ROW_TILE, third)
    attend(ck, q_t, v_t, mem_cols, dec, bounds, 2, cross_t, cross_lse, q_pair, acc)

    def fourth(r):
        rows = pl.ds(r, ROW_TILE)
        after_cross[rows, :] = after_cross[rows, :] + dot(cross_t[:, rows].T, weights[7])

    each_tile(length, ROW_TILE, fourth)


def gelu_pair(x):
    half = 0.5 * (1.0 + lax.erf(x * 0.7071067811865476))
    density = jnp.exp(x * x * -0.5) * 0.3989422804014327
    return x * half, half + x * density


def hidden_kernel(
    after_cross, cotangent, dec, expand, shrink, small, hidden_offset,
    layer_out, grad_after, d_expand, d_shrink, d_rows, d_hidden,
    small_t, low_two, low_two_t, grad_low, act, grad_pre, dec_cols,
):
    length, width = after_cross.shape
    hidden = shrink.shape[0]
    chunk = 256
    small_t[...] = small[:, :TILE].astype(F32).T
    gain, offset, last = small_t[66:67, :], small_t[67:68, :], small_t[68:69, :]
    fill_columns(dec_cols, dec)

    def keep_rows(rows):
        keep = jnp.where(dec_cols[rows, :] >= 0.0, 1.0, 0.0)
        return jnp.concatenate([keep] * (width // TILE), axis=1)

    def first(r):
        rows = pl.ds(r, ROW_TILE)
        hat, _ = normalise(after_cross[rows, :])
        low = (hat * gain + offset).astype(BF16)
        low_two[rows, :] = low
        low_two_t[:, rows] = low.T
        grad_low[rows, :] = (cotangent[rows, :].astype(F32) * keep_rows(rows)).astype(BF16)

    each_tile(length, ROW_TILE, first)

    for c in range(hidden // chunk):
        block, inside = c * chunk // width, c * chunk % width
        lanes = slice(c * chunk, (c + 1) * chunk)

        def second(i, total):
            rows = pl.ds(pl.multiple_of(i * ROW_TILE, ROW_TILE), ROW_TILE)
            pre = dot(low_two[rows, :], expand[block, :, inside : inside + chunk])
            value, slope = gelu_pair(pre + hidden_offset[:, lanes])
            act[rows, lanes] = value.astype(BF16)
            grad = (dot_nt(grad_low[rows, :], shrink[lanes, :]) * slope).astype(BF16)
            grad_pre[rows, lanes] = grad
            return total + jnp.sum(grad.astype(F32), axis=0, keepdims=True)

        d_hidden[:, lanes] = lax.fori_loop(
            0, length // ROW_TILE, second, jnp.zeros((1, chunk), F32)
        )

    d_rows[...] = jnp.zeros_like(d_rows)

    def third(r):
        rows = pl.ds(r, ROW_TILE)
        after = after_cross[rows, :]
        branch = dot(act[rows, :], shrink[...]) + last
        keep = keep_rows(rows)
        layer_out[rows, :] = (keep * (after + branch)).astype(BF16)
        low = dot_nt(grad_pre[rows, :width], expand[0])
        for j in range(1, hidden // width):
            low = low + dot_nt(grad_pre[rows, width * j : width * (j + 1)], expand[j])
        hat, rstd = normalise(after)
        out = cotangent[rows, :].astype(F32) * keep
        grad_after[rows, :] = out + norm_backward(low, hat, rstd, gain)
        d_rows[0:1, :] = d_rows[0:1, :] + jnp.sum(low * hat, axis=0, keepdims=True)
        d_rows[1:2, :] = d_rows[1:2, :] + jnp.sum(low, axis=0, keepdims=True)
        d_rows[2:3, :] = d_rows[2:3, :] + jnp.sum(out, axis=0, keepdims=True)

    each_tile(length, ROW_TILE, third)

    for j in range(hidden // width):

        def fourth(r):
            d_expand[j, pl.ds(r, TILE), :] = dot(
                low_two_t[pl.ds(r, TILE), :], grad_pre[:, width * j : width * (j + 1)]
            ).astype(BF16)

        each_tile(width, TILE, fourth)
    for c in range(hidden // chunk):
        rows = slice(c * chunk, (c + 1) * chunk)
        d_shrink[rows, :] = dot(act[:, rows].T, grad_low[...]).astype(BF16)


def backward_kernel(
    scale, shard, steps, bounds, grad_after, memory, dec, mem, weights, small,
    start, q, k, v, after_low, cq, ck, cv, mixed_t, lse, cross_t, cross_lse, d_rows, d_hidden,
    tokens_grad, memory_grad, d_attn, d_small,
    small_t, table, dec_cols, mem_cols, g, g_t, q_t, k_t, x_t, dq_t, dk, dv, d_low, e_low,
    q_rows, g_rows, q_lanes, g_lanes, acc, small_grad,
):
    length, width = start.shape
    small_t[...] = small[:, :TILE].astype(F32).T
    fill_columns(dec_cols, dec)
    fill_columns(mem_cols, mem)
    gain, offset = small_t[64:65, :], small_t[65:66, :]
    scratch = (dq_t, dk, dv, q_rows, g_rows, q_lanes, g_lanes, acc)

    def weight_grad(index, left_t, right):
        def tile(r):
            rows = pl.ds(r, TILE)
            d_attn[index, rows, :] = dot(left_t[rows, :], right[...]).astype(BF16)

        each_tile(width, TILE, tile)

    def first(r):
        rows = pl.ds(r, ROW_TILE)
        low = grad_after[rows, :].astype(BF16)
        d_low[rows, :] = low
        mixed = dot_nt(low, weights[7]).astype(BF16)
        g[rows, :] = mixed
        g_t[:, rows] = mixed.T

    each_tile(length, ROW_TILE, first)
    weight_grad(7, cross_t, d_low)
    transpose_into(q_t, cq)
    transpose_into(k_t, ck)
    attend_back(
        cq, ck, cv, g, q_t, k_t, g_t, cross_t, cross_lse, mem_cols, dec, bounds, 2, scale, *scratch
    )
    transpose_into(x_t, memory)

    def second(r):
        rows = pl.ds(r, ROW_TILE)
        key = dk[rows, :].astype(BF16)
        value = dv[rows, :].astype(BF16)
        d_low[rows, :] = key
        e_low[rows, :] = value
        memory_grad[rows, :] = dot_nt(key, weights[5]) + dot_nt(value, weights[6])

    each_tile(memory.shape[0], ROW_TILE, second)
    weight_grad(5, x_t, d_low)
    weight_grad(6, x_t, e_low)
    transpose_into(x_t, after_low)

    def third(r):
        rows = pl.ds(r, ROW_TILE)
        low = dq_t[:, rows].T
        d_low[rows, :] = low
        after = grad_after[rows, :] + dot_nt(low, weights[4])
        tokens_grad[rows, :] = after
        low = after.astype(BF16)
        e_low[rows, :] = low
        mixed = dot_nt(low, weights[3]).astype(BF16)
        g[rows, :] = mixed
        g_t[:, rows] = mixed.T

    each_tile(length, ROW_TILE, third)
    weight_grad(4, x_t, d_low)
    weight_grad(3, mixed_t, e_low)

    transpose_into(q_t, q)
    transpose_into(k_t, k)
    attend_back(
        q, k, v, g, q_t, k_t, g_t, mixed_t, lse, dec_cols, dec, bounds, 0, scale, *scratch
    )
    small_grad[...] = jnp.zeros_like(small_grad)
    table[...] = jnp.zeros_like(table)
    ids = lax.broadcasted_iota(jnp.int32, (TILE, ROW_TILE), 0).astype(F32)

    def fourth(r):
        rows = pl.ds(r, ROW_TILE)
        query = dq_t[:, rows].T
        key = dk[rows, :].astype(BF16)
        value = dv[rows, :].astype(BF16)
        g[rows, :] = query
        d_low[rows, :] = key
        e_low[rows, :] = value
        low = dot_nt(query, weights[0]) + dot_nt(key, weights[1]) + dot_nt(value, weights[2])
        hat, rstd = normalise(start[rows, :])
        normed = (hat * gain + offset).astype(BF16)
        x_t[:, rows] = normed.T
        total = tokens_grad[rows, :] + norm_backward(low, hat, rstd, gain)
        tokens_grad[rows, :] = total
        small_grad[64:65, :] = small_grad[64:65, :] + jnp.sum(low * hat, axis=0, keepdims=True)
        small_grad[65:66, :] = small_grad[65:66, :] + jnp.sum(low, axis=0, keepdims=True)
        picks = jnp.where(dec[:, rows].astype(F32) == ids, 1.0, 0.0).astype(BF16)
        high = total.astype(BF16)
        rest = (total - high.astype(F32)).astype(BF16)
        table[...] = table[...] + dot(picks, high) + dot(picks, rest)

    each_tile(length, ROW_TILE, fourth)
    weight_grad(0, x_t, g)
    weight_grad(1, x_t, d_low)
    weight_grad(2, x_t, e_low)
    for s in range(steps.shape[1]):
        row = pl.ds(steps[0, s], 1)
        small_grad[row, :] = small_grad[row, :] + table[s : s + 1, :]
    small_grad[66:69, :] = d_rows[0:3, :]
    g_f32 = small_grad[...].T
    d_small[...] = jnp.zeros_like(d_small)
    d_small[:, :TILE] = g_f32
    per_shard = d_hidden.shape[1] * shard // width
    for d in range(width // shard):
        d_small[shard * d : shard * d + 1, TILE : TILE + per_shard] = d_hidden[
            :, per_shard * d : per_shard * (d + 1)
        ]


def compute_params():
    return pltpu.CompilerParams(vmem_limit_bytes=VMEM_BYTES)


def like(*items):
    return tuple(jax.ShapeDtypeStruct(shape, kind) for shape, kind in items)


def key_bounds(dec_row, mem_row):
    def ordered(row):
        return jnp.where(row < 0, jnp.iinfo(jnp.int32).max, row)

    query = ordered(dec_row[0])
    low, high = query[::TILE], query[TILE - 1 :: TILE]
    result = []
    for row in (dec_row, mem_row):
        keys = ordered(row[0])
        before = jnp.sum((keys[None, :] < low[:, None]).astype(jnp.int32), axis=1)
        upto = jnp.sum((keys[None, :] <= high[:, None]).astype(jnp.int32), axis=1)
        result += [before // TILE, (upto + TILE - 1) // TILE]
    return jnp.stack(result)


def small_shard(time_table, vectors, expand_bias):
    rows, steps = time_table.shape
    columns = jnp.stack(vectors, axis=1)
    wide = expand_bias.shape[0]
    lead = jnp.concatenate(
        [
            jnp.pad(time_table, ((0, 0), (0, 64 - steps))),
            jnp.pad(columns, ((0, 0), (0, 64 - len(vectors)))),
        ],
        axis=1,
    )
    hidden = jnp.pad(expand_bias[None, :], ((0, rows - 1), (0, 384 - wide)))
    return jnp.concatenate([lead, hidden], axis=1)


def per_device(
    n, tokens, memory, cotangent, dec, mem, time_steps, time_table, first_gain, first_bias,
    self_query, self_key, self_value, self_out, cross_query, cross_key, cross_value, cross_out,
    second_gain, second_bias, expand_weight, expand_bias, shrink_weight, shrink_bias,
):
    _, length, width = tokens.shape
    mem_length = memory.shape[1]
    shard = self_query.shape[0]
    hidden = n * expand_bias.shape[0]
    steps_count = time_table.shape[1]
    scale = (width // HEADS) ** (-0.5)
    attn = (
        self_query, self_key, self_value, self_out, cross_query, cross_key, cross_value, cross_out
    )
    little = small_shard(
        time_table, (first_gain, first_bias, second_gain, second_bias, shrink_bias), expand_bias
    )
    direct = shard == 16
    if direct:
        one, shrink = gather_all(n, attn + (expand_weight, little, shrink_weight))
        one = one.reshape(13, width, width)
        shrink = shrink.reshape(hidden, width)
        small = one[12]
        weights, expand = one, one
    else:
        one = jnp.stack(attn + (little,) + tuple(jnp.split(expand_weight, hidden // width, axis=1)))
        one = lax.all_gather(one, "dp", axis=1, tiled=True)
        shrink = lax.all_gather(shrink_weight, "dp", axis=0, tiled=True)
        weights, small, expand = one[:8], one[8], one[9:]
    hidden_offset = (
        small.reshape(n, shard, width)[:, 0, TILE : TILE + hidden // n].reshape(1, hidden)
    ).astype(F32)
    weights, expand = one[:8], (one[8:12] if direct else expand)
    bounds = key_bounds(dec, mem)
    row_spec = [vmem_spec()] * 2
    rows = (length, width)
    mem_rows = (mem_length, width)
    (
        start, q, k, v, after_low, cq, ck, cv, mixed_t, lse, cross_t, cross_lse, after_cross
    ) = pl.pallas_call(
        functools.partial(forward_kernel, scale),
        out_shape=like(
            (rows, F32), (rows, BF16), (rows, BF16), (rows, BF16), (rows, BF16), (rows, BF16),
            (mem_rows, BF16), (mem_rows, BF16), (rows[::-1], BF16), ((HEADS, length), F32),
            (rows[::-1], BF16), ((HEADS, length), F32), (rows, F32),
        ),
        in_specs=[smem_spec()] * 2 + [vmem_spec()] * 4 + row_spec[:1] + [vmem_spec()],
        out_specs=tuple([vmem_spec()] * 13),
        scratch_shapes=[
            pltpu.VMEM((TILE, width), F32),
            pltpu.VMEM((TILE, width), F32),
            pltpu.VMEM((length, TILE), F32),
            pltpu.VMEM((mem_length, TILE), F32),
            pltpu.VMEM((width, length), BF16),
            pltpu.VMEM((width, max(length, mem_length)), BF16),
            pltpu.VMEM((width, 2 * TILE), BF16),
            pltpu.VMEM((width, TILE), F32),
        ],
        compiler_params=compute_params(),
        name="layer_forward",
    )(time_steps, bounds, tokens[0], memory[0], dec, mem, weights, small)
    layer_out, grad_after, d_expand, d_shrink, d_rows, d_hidden = pl.pallas_call(
        hidden_kernel,
        out_shape=like(
            (rows, BF16), (rows, F32), ((hidden // width, width, width), BF16),
            ((hidden, width), BF16), ((8, width), F32), ((1, hidden), F32),
        ),
        in_specs=[vmem_spec()] * 5 + [vmem_spec(), vmem_spec()],
        out_specs=tuple([vmem_spec()] * 6),
        scratch_shapes=[
            pltpu.VMEM((TILE, width), F32),
            pltpu.VMEM(rows, BF16),
            pltpu.VMEM(rows[::-1], BF16),
            pltpu.VMEM(rows, BF16),
            pltpu.VMEM((length, hidden), BF16),
            pltpu.VMEM((length, hidden), BF16),
            pltpu.VMEM((length, TILE), F32),
        ],
        compiler_params=compute_params(),
        name="hidden_layer",
    )(after_cross, cotangent[0], dec, expand, shrink, small, hidden_offset)
    both = max(length, mem_length)
    tokens_grad, memory_grad, d_attn, d_small = pl.pallas_call(
        functools.partial(backward_kernel, scale, shard),
        out_shape=like(
            (rows, F32), (mem_rows, F32), ((8, width, width), BF16), ((width, width), F32)
        ),
        in_specs=[smem_spec()] * 2 + [vmem_spec()] * 5 + [vmem_spec()]
        + [vmem_spec()] * 14,
        out_specs=tuple([vmem_spec()] * 4),
        scratch_shapes=[
            pltpu.VMEM((TILE, width), F32),
            pltpu.VMEM((TILE, width), F32),
            pltpu.VMEM((length, TILE), F32),
            pltpu.VMEM((mem_length, TILE), F32),
            pltpu.VMEM(rows, BF16),
            pltpu.VMEM(rows[::-1], BF16),
            pltpu.VMEM(rows[::-1], BF16),
            pltpu.VMEM((width, both), BF16),
            pltpu.VMEM((width, both), BF16),
            pltpu.VMEM(rows[::-1], BF16),
            pltpu.VMEM((both, width), F32),
            pltpu.VMEM((both, width), F32),
            pltpu.VMEM((both, width), BF16),
            pltpu.VMEM((both, width), BF16),
            pltpu.VMEM((width, 2 * TILE), BF16),
            pltpu.VMEM((width, 2 * TILE), BF16),
            pltpu.VMEM((2 * TILE, width), BF16),
            pltpu.VMEM((2 * TILE, width), BF16),
            pltpu.VMEM((width, TILE), F32),
            pltpu.VMEM((TILE, width), F32),
        ],
        compiler_params=compute_params(),
        name="layer_backward",
    )(
        time_steps, bounds, grad_after, memory[0], dec, mem, weights, small, start, q, k, v,
        after_low, cq, ck, cv, mixed_t, lse, cross_t, cross_lse, d_rows, d_hidden,
    )
    if direct:
        sums = scatter_sums(n, d_attn, d_expand, d_small.astype(BF16), d_shrink)
        *d_weights, d_wide, d_tall, d_little = split_sums(sums)
    else:
        totals = lax.psum_scatter(
            jnp.concatenate([d_attn, d_expand, d_small[None].astype(BF16)]).astype(F32),
            "dp", scatter_dimension=1, tiled=True,
        )
        d_tall = lax.psum_scatter(d_shrink.astype(F32), "dp", scatter_dimension=0, tiled=True)
        d_weights = [totals[j] for j in range(8)]
        d_wide = jnp.concatenate([totals[8 + j] for j in range(hidden // width)], axis=1)
        d_little = totals[-1]
    columns = [d_little[:, 64 + j] for j in range(5)]
    return (
        layer_out[None],
        tokens_grad[None],
        memory_grad[None],
        d_little[:, :steps_count],
        columns[0],
        columns[1],
        *d_weights,
        columns[2],
        columns[3],
        d_wide,
        d_little[0, TILE : TILE + hidden // n],
        d_tall,
        columns[4],
    )


def solution(mesh):
    n = mesh.shape["dp"]
    three, two, one = P("dp", None, None), P("dp", None), P("dp")
    return jax.shard_map(
        functools.partial(per_device, n),
        mesh=mesh,
        in_specs=(three,) * 3 + (two,) * 4 + (one,) * 2 + (two,) * 8 + (one,) * 2
        + (two, one, two, one),
        out_specs=(three,) * 3 + (two,) + (one,) * 2 + (two,) * 8 + (one,) * 2
        + (two, one, two, one),
        check_vma=False,
    )
```

```python
import functools

import jax
import jax.numpy as jnp
from jax import lax
from jax.experimental import pallas as pl
from jax.experimental.pallas import tpu as pltpu
from jax.sharding import PartitionSpec as P

HEADS = 8
EPS = 1e-05
NEG = -1e30
F32 = jnp.float32
BF16 = jnp.bfloat16
MESH = pl.DeviceIdType.MESH
TILE = 128
QUERY_TILE = 256
KEY_TILE = 256
SEGMENTS = 16
COUNTS = 24
VMEM_BYTES = 60 * 1024 * 1024
ROW_TILE = 256


def vmem_spec():
    return pl.BlockSpec(memory_space=pltpu.VMEM)


def smem_spec():
    return pl.BlockSpec(memory_space=pltpu.SMEM)


def hbm_spec():
    return pl.BlockSpec(memory_space=pl.ANY)


def dot(a, b):
    return lax.dot_general(a, b, (((1,), (0,)), ((), ())), preferred_element_type=F32)


def dot_tn(a, b):
    return lax.dot_general(a, b, (((0,), (0,)), ((), ())), preferred_element_type=F32)


def dot_nt(a, b):
    return lax.dot_general(a, b, (((1,), (1,)), ((), ())), preferred_element_type=F32)


class Mover:
    def __init__(self, bits, send_sem, recv_sem):
        self.bits = bits
        self.me = lax.axis_index("dp")
        self.mine = {b: lax.rem(self.me // (1 << b), 2) for b in range(bits)}
        self.sems = (send_sem, recv_sem)
        self.started = []

    def greet(self):
        for b in range(self.bits):
            pl.semaphore_signal(
                pltpu.get_barrier_semaphore(),
                inc=1,
                device_id=(self.me ^ (1 << b),),
                device_id_type=MESH,
            )

    def enter(self):
        pl.semaphore_wait(pltpu.get_barrier_semaphore(), self.bits)

    def send(self, src, dst, bit):
        i = len(self.started)
        copy = pltpu.make_async_remote_copy(
            src_ref=src,
            dst_ref=dst,
            send_sem=self.sems[0].at[i],
            recv_sem=self.sems[1].at[i],
            device_id=(self.me ^ (1 << bit),),
            device_id_type=MESH,
        )
        copy.start()
        self.started.append(copy)
        return copy

    def leave(self):
        for copy in self.started:
            copy.wait_send()

    def index(self, free, fixed, lowest=0):
        return tuple(
            slice(None) if b in free else fixed[b] for b in range(self.bits - 1, lowest - 1, -1)
        )


def link_orders(bits):
    link = list(range(bits - 1, 0, -1))
    if len(link) != 4:
        return (link, link, link)
    return ([4, 3, 2, 1], [4, 3, 1, 2], [1, 2, 4, 3])


class GatherChain:
    def __init__(self, mover, view, order):
        self.mover, self.view, self.order = mover, view, order
        self.stage = 0
        own = view(mover.index((), mover.mine))
        self.current = mover.send(own, own, order[0])
        self.inner = [mover.send(own, own, 0)]

    def advance(self):
        if self.stage == len(self.order):
            return
        mover, s = self.mover, self.stage
        self.current.wait_recv()
        if s + 1 < len(self.order):
            part = self.view(mover.index(self.order[: s + 1], mover.mine))
            self.current = mover.send(part, part, self.order[s + 1])
        other = dict(mover.mine)
        other[self.order[s]] = 1 - mover.mine[self.order[s]]
        part = self.view(mover.index(self.order[:s], other))
        self.inner.append(mover.send(part, part, 0))
        self.stage += 1

    def finish(self):
        while self.stage < len(self.order):
            self.advance()
        for copy in self.inner:
            copy.wait_recv()
        self.inner = []


class ScatterChain:
    def __init__(self, mover, source, order, arrived, work, result, steps=None):
        self.mover, self.source, self.order, self.result = mover, source, list(order), result
        self.arrived, self.work = arrived, work
        self.steps = len(order) if steps is None else steps
        self.step = 0
        self.send()

    def send(self):
        bit = self.order[self.step]
        left = sorted(self.order[self.step :], reverse=True)
        there = tuple(1 - self.mover.mine[b] if b == bit else slice(None) for b in left)
        self.current = self.mover.send(self.source(there), self.arrived[self.step], bit)

    def advance(self):
        if self.step == self.steps:
            return
        self.current.wait_recv()
        bit = self.order[self.step]
        left = sorted(self.order[self.step :], reverse=True)
        places = [()]
        for _ in left[1:]:
            places = [w + (v,) for w in places for v in (0, 1)]
        at = left.index(bit)
        arrived, work = self.arrived[self.step], self.work[self.step]
        last = self.step + 1 == self.steps
        for place in places:
            own = self.source(place[:at] + (self.mover.mine[bit],) + place[at:])[...]
            total = own.astype(F32) + arrived[place + (Ellipsis,)].astype(F32)
            if last:
                self.result(place, total)
            else:
                work[place + (Ellipsis,)] = total.astype(BF16)
        self.step += 1
        if not last:
            self.source = lambda index: work.at[index]
            self.send()


def scatter_scratch(blocks, bits, steps):
    shapes = [(blocks,) + (2,) * (bits - 1 - s) + (16, 512) for s in range(steps)]
    return [pltpu.VMEM(shape, BF16) for shape in shapes + shapes[:-1]]


def scatter_buffers(refs, slot, steps):
    arrived = [x.at[slot] for x in refs[:steps]]
    work = [x.at[slot] for x in refs[steps : 2 * steps - 1]] + [None]
    return arrived, work


def send_sems(count):
    return [pltpu.SemaphoreType.DMA((count,)), pltpu.SemaphoreType.DMA((count,))]


def pump(chains):
    for chain in chains:
        chain.advance()


def drain(chains):
    while any(chain.step < chain.steps for chain in chains):
        pump(chains)


def project_kernel(bits, scale, steps, tokens, memory, dec, *refs):
    ins, (weights, small), outs, refs = refs[:9], refs[9:11], refs[11:17], refs[17:]
    start, q, k, v, ck, cv = outs
    held, little, small_t, table, dec_cols, normed, local_sem, load_sem, send_sem, recv_sem = refs
    mover = Mover(bits, send_sem, recv_sem)
    own = mover.index((), mover.mine)
    pieces = [(ins[8], small.at[(0,) + own])]
    pieces += [(ins[j], weights.at[(j,) + own]) for j in range(8)]
    local = [pltpu.make_async_copy(s, d, local_sem.at[i]) for i, (s, d) in enumerate(pieces)]
    for copy in local:
        copy.start()
    mover.greet()
    fill_columns(dec_cols, dec)
    mover.enter()
    for copy in local:
        copy.wait()
    a, b, c = link_orders(bits)

    def block(buf, j, order):
        return GatherChain(mover, lambda index: buf.at[(j,) + index], order)

    first = [
        block(small, 0, c),
        block(weights, 0, a),
        block(weights, 1, b),
        block(weights, 2, c),
    ]
    rest = [
        block(weights, 5, a),
        block(weights, 6, b),
        block(weights, 3, a),
        block(weights, 4, b),
        block(weights, 7, c),
    ]
    for _ in range(4):
        pump(first)
        pump(rest)

    def load(i, src, dst):
        copy = pltpu.make_async_copy(src, dst, load_sem.at[i])
        copy.start()
        return copy

    for chain in first:
        chain.finish()
    loads = [load(3, small.at[0], little)] + [load(j, weights.at[j], held.at[j]) for j in range(3)]
    pump(rest)
    loads[0].wait()
    width = tokens.shape[1]
    small_t[...] = little[...].reshape(width, width)[:, :TILE].astype(F32).T
    begin_rows(steps, tokens, start, normed, small_t, table, dec_cols)
    for copy in loads[1:]:
        copy.wait()
    q[...] = (dot(normed[...], held[0].reshape(width, width)) * scale).astype(BF16)
    pump(rest)
    k[...] = dot(normed[...], held[1].reshape(width, width)).astype(BF16)
    v[...] = dot(normed[...], held[2].reshape(width, width)).astype(BF16)
    for chain in rest[:2]:
        chain.finish()
    loads = [load(j, weights.at[5 + j], held.at[j]) for j in range(2)]
    for copy in loads:
        copy.wait()
    ck[...] = dot(memory[...], held[0].reshape(width, width)).astype(BF16)
    cv[...] = dot(memory[...], held[1].reshape(width, width)).astype(BF16)
    for chain in rest[2:]:
        chain.finish()
    mover.leave()


def project(n, scale, steps, tokens, memory, dec, arrays):
    bits = n.bit_length() - 1
    two = (2,) * bits
    length, width = tokens.shape
    mem_length = memory.shape[0]
    return pl.pallas_call(
        functools.partial(project_kernel, bits, scale),
        out_shape=like(
            ((8,) + two + (16, 512), BF16),
            ((1,) + two + (16, 512), BF16),
            ((length, width), F32),
            ((length, width), BF16),
            ((length, width), BF16),
            ((length, width), BF16),
            ((mem_length, width), BF16),
            ((mem_length, width), BF16),
        ),
        in_specs=[smem_spec()] + [vmem_spec()] * 12,
        out_specs=(hbm_spec(),) * 2 + (vmem_spec(),) * 6,
        scratch_shapes=[
            pltpu.VMEM((3,) + two + (16, 512), BF16),
            pltpu.VMEM(two + (16, 512), BF16),
            pltpu.VMEM((TILE, width), F32),
            pltpu.VMEM((TILE, width), F32),
            pltpu.VMEM((length, TILE), F32),
            pltpu.VMEM((length, width), BF16),
            pltpu.SemaphoreType.DMA((9,)),
            pltpu.SemaphoreType.DMA((4,)),
        ]
        + send_sems(9 * (2 * bits - 1)),
        compiler_params=pltpu.CompilerParams(
            collective_id=0, has_side_effects=True, vmem_limit_bytes=VMEM_BYTES
        ),
        name="gather_project",
    )(steps, tokens, memory, dec, *arrays)


def scatter_kernel(bits, attn, little, carried, out, hidden_out, *refs):
    buffers, resumed, (send_sem, recv_sem) = (
        refs[: 2 * bits - 1], refs[2 * bits - 1 : -2], refs[-2:]
    )
    mover = Mover(bits, send_sem, recv_sem)
    mover.greet()
    mover.enter()
    orders = scatter_orders(bits)

    def keep(ref, slot):
        def result(place, total):
            ref[slot] = total

        return result

    chains = []
    for j in range(9):
        ref, inside = (attn, j) if j < 8 else (little, 0)
        chains.append(
            ScatterChain(
                mover,
                lambda index, ref=ref, inside=inside: ref.at[(inside,) + index],
                (0,) + orders[j % 8],
                *scatter_buffers(buffers, j, bits),
                keep(out, j),
            )
        )
    for j in range(hidden_out.shape[0]):
        chains.append(
            ScatterChain(
                mover,
                lambda index, j=j: carried.at[(j,) + index],
                orders[j % 8][1:],
                *scatter_buffers(resumed, j, bits - 2),
                keep(hidden_out, j),
            )
        )
    drain(chains)
    mover.leave()


def scatter_orders(bits):
    a, b, c = (tuple(order[::-1]) for order in link_orders(bits))
    return (a, b, c, a, b, a, b, c)


def scatter_sums(n, attn, little, carried):
    bits = n.bit_length() - 1
    two = (2,) * bits
    blocks = carried.shape[0]
    return pl.pallas_call(
        functools.partial(scatter_kernel, bits),
        out_shape=like(((9, 16, 512), F32), ((blocks, 16, 512), F32)),
        in_specs=[vmem_spec()] * 3,
        out_specs=(vmem_spec(),) * 2,
        scratch_shapes=scatter_scratch(9, bits, bits)
        + scatter_scratch(blocks, bits - 2, bits - 2)
        + send_sems(9 * bits + blocks * (bits - 2)),
        compiler_params=pltpu.CompilerParams(
            collective_id=1, has_side_effects=True, vmem_limit_bytes=VMEM_BYTES
        ),
        name="scatter_sums",
    )(attn.reshape((8,) + two + (16, 512)), little.reshape((1,) + two + (16, 512)), carried)


def split_kernel(sums, hidden_sums, *outs):
    for j in range(8):
        outs[j][...] = sums[j]
    for j in range(4):
        outs[8][:, 512 * j : 512 * (j + 1)] = hidden_sums[j]
        outs[9][16 * j : 16 * (j + 1), :] = hidden_sums[4 + j]
    little = sums[8]
    outs[10][...] = little[:, : outs[10].shape[1]]
    turned = little[:, :TILE].T
    for j in range(5):
        outs[11 + j][...] = turned[64 + j, :16]
    outs[16][...] = little[0, TILE : TILE + 64]


def split_sums(sums, hidden_sums, steps):
    shapes = [(16, 512)] * 8 + [(16, 2048), (64, 512), (16, steps)] + [(16,)] * 5 + [(64,)]
    return pl.pallas_call(
        split_kernel,
        out_shape=tuple(jax.ShapeDtypeStruct(shape, F32) for shape in shapes),
        in_specs=[vmem_spec()] * 2,
        out_specs=tuple([vmem_spec()] * len(shapes)),
        name="split_sums",
    )(sums, hidden_sums)


def each_tile(length, size, body):
    def step(i, carry):
        body(pl.multiple_of(i * size, size))
        return carry

    lax.fori_loop(0, length // size, step, 0)


def fill_columns(target, row_ref):
    for r in range(0, row_ref.shape[1], TILE):
        row = row_ref[:, r : r + TILE].astype(F32)
        target[r : r + TILE, :] = jnp.broadcast_to(row, (TILE, TILE)).T


def normalise(x):
    centred = x - jnp.mean(x, axis=-1, keepdims=True)
    rstd = lax.rsqrt(jnp.mean(centred * centred, axis=-1, keepdims=True) + EPS)
    return centred * rstd, rstd


def norm_backward(grad, hat, rstd, gain):
    scaled = grad * gain
    first = jnp.mean(scaled, axis=-1, keepdims=True)
    second = jnp.mean(scaled * hat, axis=-1, keepdims=True)
    return rstd * (scaled - first - hat * second)


def pair_columns(target, block):
    even = (lax.broadcasted_iota(jnp.int32, block.shape, 0) & 64) == 0
    zero = jnp.zeros_like(block)
    target[:, : block.shape[1]] = jnp.where(even, block, zero)
    target[:, block.shape[1] :] = jnp.where(even, zero, block)


def pair_rows(target, block):
    even = (lax.broadcasted_iota(jnp.int32, block.shape, 1) & 64) == 0
    zero = jnp.zeros_like(block)
    target[: block.shape[0], :] = jnp.where(even, block, zero)
    target[block.shape[0] :, :] = jnp.where(even, zero, block)


def band_bias(key_cols, there, seg_q):
    cols = key_cols[there, :]
    parts = [
        jnp.where(cols == seg_q[:, TILE * j : TILE * (j + 1)], 0.0, NEG)
        for j in range(QUERY_TILE // TILE)
    ]
    return jnp.concatenate(parts + parts, axis=1)


def stacked(pair):
    return jnp.concatenate([pair[:, :QUERY_TILE], pair[:, QUERY_TILE:]], axis=0)


def key_tile(kb):
    return pl.ds(pl.multiple_of(kb * KEY_TILE, KEY_TILE), KEY_TILE)


def count_below(target, row_ref, first):
    row = row_ref[...].astype(F32)
    row = jnp.where(row < 0.0, float(SEGMENTS), row)
    ids = lax.broadcasted_iota(jnp.int32, (COUNTS, row.shape[1]), 0).astype(F32)
    total = jnp.sum(jnp.where(row < ids, 1.0, 0.0), axis=1, keepdims=True)
    target[first : first + COUNTS, :] = jnp.broadcast_to(total, (COUNTS, TILE)).astype(jnp.int32)


def fill_bounds(bounds, counts, dec_ids):
    for i in range(dec_ids.shape[1] // QUERY_TILE):
        low = dec_ids[0, i * QUERY_TILE]
        high = dec_ids[0, (i + 1) * QUERY_TILE - 1]
        low = jnp.where(low < 0, SEGMENTS, low)
        high = jnp.where(high < 0, SEGMENTS, high)
        for j in range(2):
            bounds[2 * j, i] = counts[COUNTS * j + low, 0] // KEY_TILE
            bounds[2 * j + 1, i] = (
                counts[COUNTS * j + high + 1, 0] + KEY_TILE - 1
            ) // KEY_TILE


def attend(k, v, q_t, key_cols, query_row, bounds, which, out, lse, q_pair, v_pair, held, acc):
    width = out.shape[1]
    pairs = width // TILE

    def query_block(q0):
        i = q0 // QUERY_TILE
        here = pl.ds(q0, QUERY_TILE)
        low, high = bounds[which, i], bounds[which + 1, i]
        pair_columns(q_pair, q_t[:, here])
        seg_q = query_row[:, here].astype(F32)

        def score(kb, carry):
            there = key_tile(kb)
            bias = band_bias(key_cols, there, seg_q)
            result = []
            for p in range(pairs):
                lanes = slice(TILE * p, TILE * (p + 1))
                top, total = carry[p]
                scores = dot(k[there, lanes], q_pair[lanes, :]) + bias
                held[kb, p] = scores
                now = jnp.maximum(top, jnp.max(scores, axis=0, keepdims=True))
                added = jnp.sum(jnp.exp(scores - now), axis=0, keepdims=True)
                result.append((now, total * jnp.exp(top - now) + added))
            return tuple(result)

        begin = tuple(
            (jnp.full((1, 2 * QUERY_TILE), NEG, F32), jnp.zeros((1, 2 * QUERY_TILE), F32))
            for _ in range(pairs)
        )
        levels = [top + jnp.log(total) for top, total in lax.fori_loop(low, high, score, begin)]
        for p in range(pairs):
            lse[2 * p : 2 * p + 1, here] = levels[p][:, :QUERY_TILE]
            lse[2 * p + 1 : 2 * p + 2, here] = levels[p][:, QUERY_TILE:]
        acc[...] = jnp.zeros_like(acc)

        def mix(kb, carry):
            pair_rows(v_pair, v[key_tile(kb), :])
            for p in range(pairs):
                lanes = slice(TILE * p, TILE * (p + 1))
                probs = jnp.exp(held[kb, p] - levels[p]).astype(BF16)
                acc[:, lanes] = acc[:, lanes] + dot_tn(stacked(probs), v_pair[:, lanes])
            return carry

        lax.fori_loop(low, high, mix, 0)
        out[here, :] = acc[...].astype(BF16)

    each_tile(q_t.shape[1], QUERY_TILE, query_block)


def attend_back(
    q, k, v, g, q_t, k_t, g_t, out_t, lse, key_cols, query_row, bounds, which, scale,
    dq, dk, dv, q_cols, g_cols, q_pair, g_pair, acc,
):
    width = q.shape[1]
    pairs = width // TILE
    dk[...] = jnp.zeros_like(dk)
    dv[...] = jnp.zeros_like(dv)

    def query_block(q0):
        i = q0 // QUERY_TILE
        here = pl.ds(q0, QUERY_TILE)
        pair_columns(q_cols, q_t[:, here])
        pair_columns(g_cols, g_t[:, here])
        pair_rows(q_pair, q[here, :])
        pair_rows(g_pair, g[here, :])
        seg_q = query_row[:, here].astype(F32)
        acc[...] = jnp.zeros_like(acc)
        centres, levels = [], []
        for p in range(pairs):
            both = []
            for h in range(2):
                rows = slice(TILE * p + 64 * h, TILE * p + 64 * (h + 1))
                product = g_t[rows, here].astype(F32) * out_t[rows, here].astype(F32)
                both.append(jnp.sum(product, axis=0, keepdims=True))
            centres.append(jnp.concatenate(both, axis=1))
            levels.append(
                jnp.concatenate(
                    [lse[2 * p : 2 * p + 1, here], lse[2 * p + 1 : 2 * p + 2, here]], axis=1
                )
            )

        def key_block(kb, carry):
            there = key_tile(kb)
            bias = band_bias(key_cols, there, seg_q)
            for p in range(pairs):
                lanes = slice(TILE * p, TILE * (p + 1))
                scores = dot(k[there, lanes], q_cols[lanes, :]) + bias
                probs = jnp.exp(scores - levels[p])
                grads = dot(v[there, lanes], g_cols[lanes, :])
                low = (probs * (grads - centres[p])).astype(BF16)
                dv[there, lanes] = dv[there, lanes] + dot(probs.astype(BF16), g_pair[:, lanes])
                dk[there, lanes] = dk[there, lanes] + dot(low, q_pair[:, lanes])
                for h in range(2):
                    rows = slice(TILE * p + 64 * h, TILE * p + 64 * (h + 1))
                    cols = slice(QUERY_TILE * h, QUERY_TILE * (h + 1))
                    acc[rows, :] = acc[rows, :] + dot(k_t[rows, there], low[:, cols])
            return carry

        lax.fori_loop(bounds[which, i], bounds[which + 1, i], key_block, 0)
        dq[here, :] = (acc[...] * scale).T.astype(BF16)

    each_tile(q_t.shape[1], QUERY_TILE, query_block)


def project_alone_kernel(
    scale, steps, tokens, memory, dec, weights, small, start, q, k, v, ck, cv,
    small_t, table, dec_cols, normed,
):
    fill_columns(dec_cols, dec)
    small_t[...] = small[:, :TILE].astype(F32).T
    begin_rows(steps, tokens, start, normed, small_t, table, dec_cols)
    q[...] = (dot(normed[...], weights[0]) * scale).astype(BF16)
    k[...] = dot(normed[...], weights[1]).astype(BF16)
    v[...] = dot(normed[...], weights[2]).astype(BF16)
    ck[...] = dot(memory[...], weights[5]).astype(BF16)
    cv[...] = dot(memory[...], weights[6]).astype(BF16)


def begin_rows(steps, tokens, start, normed, small_t, table, dec_cols):
    table[...] = jnp.zeros_like(table)
    for s in range(steps.shape[1]):
        table[s : s + 1, :] = small_t[pl.ds(steps[0, s], 1), :]
    gain, offset = small_t[64:65, :], small_t[65:66, :]

    def begin(r):
        rows = pl.ds(r, ROW_TILE)
        ids = lax.broadcasted_iota(jnp.int32, (ROW_TILE, TILE), 1).astype(F32)
        picks = jnp.where(dec_cols[rows, :] == ids, 1.0, 0.0).astype(BF16)
        value = tokens[rows, :].astype(F32) + dot(picks, table[...].astype(BF16))
        start[rows, :] = value
        hat, _ = normalise(value)
        normed[rows, :] = (hat * gain + offset).astype(BF16)

    each_tile(tokens.shape[0], ROW_TILE, begin)


def forward_kernel(
    scale, dec_ids, dec, mem, weights, start, q, k, v, ck, cv,
    bounds, after_low, cq, mixed, lse, cross, cross_lse, after_cross,
    counts, counted, count_sem, dec_cols, mem_cols, q_t, q_pair, v_pair, held, acc,
):
    count_below(counts, dec, 0)
    count_below(counts, mem, COUNTS)
    copy = pltpu.make_async_copy(counts, counted, count_sem)
    copy.start()
    fill_columns(dec_cols, dec)
    fill_columns(mem_cols, mem)
    q_t[...] = q[...].T
    copy.wait()
    fill_bounds(bounds, counted, dec_ids)
    work = (q_pair, v_pair, held, acc)
    attend(k, v, q_t, dec_cols, dec, bounds, 0, mixed, lse, *work)
    after = start[...] + dot(mixed[...], weights[3])
    after_cross[...] = after
    low = after.astype(BF16)
    after_low[...] = low
    query = (dot(low, weights[4]) * scale).astype(BF16)
    cq[...] = query
    q_t[...] = query.T
    attend(ck, cv, q_t, mem_cols, dec, bounds, 2, cross, cross_lse, *work)
    after_cross[...] = after_cross[...] + dot(cross[...], weights[7])


def gelu_pair(x):
    half = 0.5 * (1.0 + lax.erf(x * 0.7071067811865476))
    density = jnp.exp(x * x * -0.5) * 0.3989422804014327
    return x * half, half + x * density


def hidden_kernel(
    shard, bits, after_cross, cotangent, dec, small, *refs,
):
    if bits:
        packed, refs = refs[0], refs[1:]
    else:
        (expand, shrink), refs = refs[:2], refs[2:]
    (layer_out, grad_after, d_rows, d_hidden), refs = refs[:4], refs[4:]
    if bits:
        sums, expand, shrink, load_sem, refs = *refs[:4], refs[4:]
        load = [
            pltpu.make_async_copy(
                packed.at[:, pl.ds(16 * j, 16)], expand.at[j], load_sem.at[j]
            )
            for j in range(expand.shape[0])
        ] + [
            pltpu.make_async_copy(
                packed.at[:, pl.ds(16 * expand.shape[0], shrink.shape[1])], shrink, load_sem.at[4]
            )
        ]
        for copy in load:
            copy.start()
    (d_expand, d_shrink), refs = refs[:2], refs[2:]
    (small_t, hidden_offset, wide, low_two, grad_low, act, grad_pre, dec_cols), refs = (
        refs[:8], refs[8:]
    )
    length, width = after_cross.shape
    hidden = act.shape[1]
    blocks = hidden // width
    chains = []
    if bits:
        buffers = refs[:-2]
        mover = Mover(bits, *refs[-2:])
        mover.greet()
        orders = scatter_orders(bits)

    def wide_weight(j):
        return expand[j].reshape(width, width)

    def tall_weight(first, last):
        if not bits:
            return shrink[first:last, :]
        tall = shrink.shape[1]
        return shrink[first // tall : last // tall].reshape(last - first, width)

    def step():
        for chain in chains:
            if chain.step == 0:
                chain.advance()

    def start_chain(view, slot):
        def result(place, total):
            sums[(slot,) + place] = total.astype(BF16)

        chains.append(
            ScatterChain(
                mover, view, (0,) + orders[slot % 8], *scatter_buffers(buffers, slot, 2), result, 2
            )
        )

    small_t[...] = small[:, :TILE].astype(F32).T
    wide[...] = small[:, TILE : 2 * TILE].astype(F32)
    per_shard = hidden * shard // width
    for d in range(width // shard):
        hidden_offset[:, per_shard * d : per_shard * (d + 1)] = wide[
            shard * d : shard * d + 1, :per_shard
        ]
    gain, offset, last = small_t[66:67, :], small_t[67:68, :], small_t[68:69, :]
    fill_columns(dec_cols, dec)

    def keep_rows(rows):
        keep = jnp.where(dec_cols[rows, :] >= 0.0, 1.0, 0.0)
        return jnp.concatenate([keep] * (width // TILE), axis=1)

    def first(r):
        rows = pl.ds(r, ROW_TILE)
        hat, _ = normalise(after_cross[rows, :])
        low_two[rows, :] = (hat * gain + offset).astype(BF16)
        grad_low[rows, :] = (cotangent[rows, :].astype(F32) * keep_rows(rows)).astype(BF16)

    each_tile(length, ROW_TILE, first)
    if bits:
        for copy in load:
            copy.wait()

    for j in range(blocks):
        lanes = slice(width * j, width * (j + 1))
        value, slope = gelu_pair(dot(low_two[...], wide_weight(j)) + hidden_offset[:, lanes])
        act[:, lanes] = value.astype(BF16)
        grad = (dot_nt(grad_low[...], tall_weight(lanes.start, lanes.stop)) * slope).astype(BF16)
        grad_pre[:, lanes] = grad
        d_hidden[:, lanes] = jnp.sum(grad.astype(F32), axis=0, keepdims=True)
        if bits and j == 0:
            mover.enter()
        step()
        part = dot_tn(low_two[...], grad_pre[:, lanes]).astype(BF16)
        d_expand[j] = part.reshape(d_expand.shape[1:])
        if bits:
            start_chain(lambda index, j=j: d_expand.at[(j,) + index], j)
    for j in range(blocks):
        lanes = slice(width * j, width * (j + 1))
        part = dot_tn(act[:, lanes], grad_low[...]).astype(BF16)
        if bits:
            owners = width // d_shrink.shape[-2]
            part = part.reshape((owners,) + d_shrink.shape[-2:])
            lead = mover.bits - owners.bit_length() + 1
            first_bits = [(j >> (lead - 1 - i)) & 1 for i in range(lead)]
            d_shrink[tuple(first_bits)] = part.reshape(d_shrink.shape[lead:])
        else:
            d_shrink[lanes, :] = part
    step()
    if bits:
        for j in range(blocks):
            start_chain(
                lambda index, j=j: d_shrink.at[index + (slice(16 * j, 16 * (j + 1)),)],
                blocks + j,
            )

    d_rows[...] = jnp.zeros_like(d_rows)
    for half in (slice(0, length // 2), slice(length // 2, length)):
        grad_after[half, :] = dot(act[half, :], tall_weight(0, hidden))
        step()

    def third(r):
        rows = pl.ds(r, ROW_TILE)
        keep = keep_rows(rows)
        layer_out[rows, :] = (keep * (after_cross[rows, :] + grad_after[rows, :] + last)).astype(
            BF16
        )

    each_tile(length, ROW_TILE, third)
    step()
    for half in (slice(0, length // 2), slice(length // 2, length)):
        low = dot_nt(grad_pre[half, :width], wide_weight(0))
        for j in range(1, blocks):
            low = low + dot_nt(grad_pre[half, width * j : width * (j + 1)], wide_weight(j))
        grad_after[half, :] = low
        step()

    def fourth(r):
        rows = pl.ds(r, ROW_TILE)
        low = grad_after[rows, :]
        hat, rstd = normalise(after_cross[rows, :])
        out = cotangent[rows, :].astype(F32) * keep_rows(rows)
        grad_after[rows, :] = out + norm_backward(low, hat, rstd, gain)
        d_rows[0:1, :] = d_rows[0:1, :] + jnp.sum(low * hat, axis=0, keepdims=True)
        d_rows[1:2, :] = d_rows[1:2, :] + jnp.sum(low, axis=0, keepdims=True)
        d_rows[2:3, :] = d_rows[2:3, :] + jnp.sum(out, axis=0, keepdims=True)

    each_tile(length, ROW_TILE, fourth)
    if bits:
        drain(chains)
        mover.leave()


def backward_kernel(
    scale, shard, steps, bounds, grad_after, memory, dec, mem, weights, small,
    start, q, k, v, after_low, cq, ck, cv, mixed, lse, cross, cross_lse, d_rows, d_hidden,
    layer_part, tokens_grad, memory_grad, d_attn, d_small, layer_out, layer_sem,
    small_t, table, dec_cols, mem_cols, g, g_t, q_t, k_t, out_t, dq, dk, dv, d_low, e_low,
    q_cols, g_cols, q_pair, g_pair, acc, small_grad, wide,
):
    length, width = start.shape
    passed = pltpu.make_async_copy(layer_part, layer_out, layer_sem)
    passed.start()
    small_t[...] = small[:, :TILE].astype(F32).T
    fill_columns(dec_cols, dec)
    fill_columns(mem_cols, mem)
    gain, offset = small_t[64:65, :], small_t[65:66, :]
    work = (dq, dk, dv, q_cols, g_cols, q_pair, g_pair, acc)

    def weight_grad(index, left, right):
        d_attn[index] = dot_tn(left[...], right[...]).astype(BF16)

    d_low[...] = grad_after[...].astype(BF16)
    mixed_grad = dot_nt(d_low[...], weights[7]).astype(BF16)
    g[...] = mixed_grad
    g_t[...] = mixed_grad.T
    weight_grad(7, cross, d_low)
    q_t[...] = cq[...].T
    k_t[...] = ck[...].T
    out_t[...] = cross[...].T
    attend_back(
        cq, ck, cv, g, q_t, k_t, g_t, out_t, cross_lse, mem_cols, dec, bounds, 2, scale, *work
    )
    d_low[...] = dk[...].astype(BF16)
    e_low[...] = dv[...].astype(BF16)
    memory_grad[...] = dot_nt(d_low[...], weights[5]) + dot_nt(e_low[...], weights[6])
    weight_grad(5, memory, d_low)
    weight_grad(6, memory, e_low)
    after = grad_after[...] + dot_nt(dq[...], weights[4])
    weight_grad(4, after_low, dq)
    tokens_grad[...] = after
    d_low[...] = after.astype(BF16)
    mixed_grad = dot_nt(d_low[...], weights[3]).astype(BF16)
    g[...] = mixed_grad
    g_t[...] = mixed_grad.T
    weight_grad(3, mixed, d_low)

    q_t[...] = q[...].T
    k_t[...] = k[...].T
    out_t[...] = mixed[...].T
    attend_back(q, k, v, g, q_t, k_t, g_t, out_t, lse, dec_cols, dec, bounds, 0, scale, *work)
    d_low[...] = dk[...].astype(BF16)
    e_low[...] = dv[...].astype(BF16)
    dk[...] = (
        dot_nt(dq[...], weights[0]) + dot_nt(d_low[...], weights[1]) + dot_nt(e_low[...], weights[2])
    )
    small_grad[...] = jnp.zeros_like(small_grad)
    table[...] = jnp.zeros_like(table)
    ids = lax.broadcasted_iota(jnp.int32, (TILE, ROW_TILE), 0).astype(F32)

    def last(r):
        rows = pl.ds(r, ROW_TILE)
        low = dk[rows, :]
        hat, rstd = normalise(start[rows, :])
        g[rows, :] = (hat * gain + offset).astype(BF16)
        total = tokens_grad[rows, :] + norm_backward(low, hat, rstd, gain)
        tokens_grad[rows, :] = total
        small_grad[64:65, :] = small_grad[64:65, :] + jnp.sum(low * hat, axis=0, keepdims=True)
        small_grad[65:66, :] = small_grad[65:66, :] + jnp.sum(low, axis=0, keepdims=True)
        picks = jnp.where(dec[:, rows].astype(F32) == ids, 1.0, 0.0).astype(BF16)
        high = total.astype(BF16)
        rest = (total - high.astype(F32)).astype(BF16)
        table[...] = table[...] + dot(picks, high) + dot(picks, rest)

    each_tile(length, ROW_TILE, last)
    weight_grad(0, g, dq)
    weight_grad(1, g, d_low)
    weight_grad(2, g, e_low)
    for s in range(steps.shape[1]):
        row = pl.ds(steps[0, s], 1)
        small_grad[row, :] = small_grad[row, :] + table[s : s + 1, :]
    small_grad[66:69, :] = d_rows[0:3, :]
    d_small[...] = jnp.zeros_like(d_small)
    d_small[:, :TILE] = small_grad[...].T.astype(BF16)
    wide[...] = jnp.zeros_like(wide)
    per_shard = d_hidden.shape[1] * shard // width
    for d in range(width // shard):
        wide[shard * d : shard * d + 1, :per_shard] = d_hidden[
            :, per_shard * d : per_shard * (d + 1)
        ]
    d_small[:, TILE : 2 * TILE] = wide[...].astype(BF16)
    passed.wait()


def compute_params():
    return pltpu.CompilerParams(vmem_limit_bytes=VMEM_BYTES)


def like(*items):
    return tuple(jax.ShapeDtypeStruct(shape, kind) for shape, kind in items)


def pack_kernel(table, expand, expand_bias, shrink, *refs):
    vectors, (packed, little, turned) = refs[:5], refs[5:]
    rows, width = little.shape
    for j in range(expand.shape[1] // width):
        packed[rows * j : rows * (j + 1), :] = expand[:, width * j : width * (j + 1)]
    packed[packed.shape[0] - shrink.shape[0] :, :] = shrink[...]
    turned[...] = jnp.zeros_like(turned)
    for j in range(5):
        turned[64 + j : 65 + j, :rows] = vectors[j][...].astype(F32).reshape(1, rows)
    columns = turned[...].T
    little[...] = jnp.zeros_like(little)
    turned[:rows, :] = columns[:rows, :]
    turned[:rows, : table.shape[1]] = table[...].astype(F32)
    little[:, :TILE] = turned[:rows, :].astype(BF16)
    turned[:rows, :] = jnp.zeros((rows, TILE), F32)
    wide = expand_bias.shape[0]
    turned[:1, :wide] = expand_bias[...].astype(F32).reshape(1, wide)
    little[:, TILE : 2 * TILE] = turned[:rows, :].astype(BF16)


def pack(table, expand, expand_bias, shrink, vectors):
    rows, width = table.shape[0], shrink.shape[1]
    packed_rows = rows * (expand.shape[1] // width) + shrink.shape[0]
    return pl.pallas_call(
        pack_kernel,
        out_shape=like(((packed_rows, width), BF16), ((rows, width), BF16)),
        in_specs=[vmem_spec()] * 9,
        out_specs=(vmem_spec(),) * 2,
        scratch_shapes=[pltpu.VMEM((TILE, TILE), F32)],
        name="pack_shard",
    )(table, expand, expand_bias, shrink, *vectors)


def per_device(
    n, tokens, memory, cotangent, dec, mem, time_steps, time_table, first_gain, first_bias,
    self_query, self_key, self_value, self_out, cross_query, cross_key, cross_value, cross_out,
    second_gain, second_bias, expand_weight, expand_bias, shrink_weight, shrink_bias,
):
    _, length, width = tokens.shape
    mem_length = memory.shape[1]
    shard = self_query.shape[0]
    hidden = n * expand_bias.shape[0]
    steps_count = time_table.shape[1]
    scale = (width // HEADS) ** (-0.5)
    attn = (
        self_query, self_key, self_value, self_out, cross_query, cross_key, cross_value, cross_out
    )
    packed, little = pack(
        time_table,
        expand_weight,
        expand_bias,
        shrink_weight,
        (first_gain, first_bias, second_gain, second_bias, shrink_bias),
    )
    direct = shard == 16
    bits = n.bit_length() - 1 if direct else 0
    rows = (length, width)
    mem_rows = (mem_length, width)
    projected = [(rows, F32)] + [(rows, BF16)] * 3 + [(mem_rows, BF16)] * 2
    if direct:
        hidden_weights = (lax.all_gather(packed, "dp"),)
        weights, small, start, q, k, v, ck, cv = project(
            n, scale, time_steps, tokens[0], memory[0], dec, attn + (little,)
        )
        weights = weights.reshape(8, width, width)
        small = small.reshape(width, width)
    else:
        one = jnp.stack(attn + (little,) + tuple(jnp.split(expand_weight, hidden // width, axis=1)))
        one = lax.all_gather(one, "dp", axis=1, tiled=True)
        shrink = lax.all_gather(shrink_weight, "dp", axis=0, tiled=True)
        weights, small, hidden_weights = one[:8], one[8], (one[9:], shrink)
        start, q, k, v, ck, cv = pl.pallas_call(
            functools.partial(project_alone_kernel, scale),
            out_shape=like(*projected),
            in_specs=[smem_spec()] + [vmem_spec()] * 5,
            out_specs=(vmem_spec(),) * 6,
            scratch_shapes=[
                pltpu.VMEM((TILE, width), F32),
                pltpu.VMEM((TILE, width), F32),
                pltpu.VMEM((length, TILE), F32),
                pltpu.VMEM(rows, BF16),
            ],
            compiler_params=compute_params(),
            name="project",
        )(time_steps, tokens[0], memory[0], dec, weights, small)
    both = max(length, mem_length)
    stats = (HEADS, length)
    bounds, after_low, cq, mixed, lse, cross, cross_lse, after_cross = pl.pallas_call(
        functools.partial(forward_kernel, scale),
        out_shape=like(
            ((4, length // QUERY_TILE), jnp.int32),
            (rows, BF16), (rows, BF16), (rows, BF16), (stats, F32),
            (rows, BF16), (stats, F32), (rows, F32),
        ),
        in_specs=[smem_spec()] + [vmem_spec()] * 9,
        out_specs=(smem_spec(),) + tuple([vmem_spec()] * 7),
        scratch_shapes=[
            pltpu.VMEM((2 * COUNTS, TILE), jnp.int32),
            pltpu.SMEM((2 * COUNTS, TILE), jnp.int32),
            pltpu.SemaphoreType.DMA,
            pltpu.VMEM((length, TILE), F32),
            pltpu.VMEM((mem_length, TILE), F32),
            pltpu.VMEM(rows[::-1], BF16),
            pltpu.VMEM((width, 2 * QUERY_TILE), BF16),
            pltpu.VMEM((2 * KEY_TILE, width), BF16),
            pltpu.VMEM((both // KEY_TILE, width // TILE, KEY_TILE, 2 * QUERY_TILE), F32),
            pltpu.VMEM((QUERY_TILE, width), F32),
        ],
        compiler_params=compute_params(),
        name="layer_forward",
    )(dec, dec, mem, weights, start, q, k, v, ck, cv)
    blocks = hidden // width
    partial = [
        ((blocks,) + ((2,) * bits + (16, 512) if direct else (width, width)), BF16),
        ((2,) * bits + (64, 512) if direct else (hidden, width), BF16),
    ]
    results = [((2 * blocks,) + (2,) * (bits - 2) + (16, 512), BF16)] if direct else partial
    loaded = [
        pltpu.VMEM((blocks, n, shard, width), BF16),
        pltpu.VMEM((n, hidden // n, width), BF16),
        pltpu.SemaphoreType.DMA((blocks + 1,)),
    ]
    held = loaded + [pltpu.VMEM(*item) for item in partial] if direct else []
    layer_part, grad_after, d_rows, d_hidden, *hidden_sums = pl.pallas_call(
        functools.partial(hidden_kernel, shard, bits),
        out_shape=like(
            (rows, BF16), (rows, F32), ((8, width), F32), ((1, hidden), F32), *results
        ),
        in_specs=[vmem_spec()] * 4 + ([hbm_spec()] if direct else [vmem_spec()] * 2),
        out_specs=tuple([vmem_spec()] * (4 + len(results))),
        scratch_shapes=held + [
            pltpu.VMEM((TILE, width), F32),
            pltpu.VMEM((1, hidden), F32),
            pltpu.VMEM((width, TILE), F32),
            pltpu.VMEM(rows, BF16),
            pltpu.VMEM(rows, BF16),
            pltpu.VMEM((length, hidden), BF16),
            pltpu.VMEM((length, hidden), BF16),
            pltpu.VMEM((length, TILE), F32),
        ] + (scatter_scratch(2 * blocks, bits, 2) + send_sems(4 * blocks) if direct else []),
        compiler_params=pltpu.CompilerParams(
            collective_id=2, has_side_effects=True, vmem_limit_bytes=VMEM_BYTES
        ) if direct else compute_params(),
        name="hidden_layer",
    )(after_cross, cotangent[0], dec, small, *hidden_weights)
    tokens_grad, memory_grad, d_attn, d_small, layer_out = pl.pallas_call(
        functools.partial(backward_kernel, scale, shard),
        out_shape=like(
            (rows, F32), (mem_rows, F32), ((8, width, width), BF16), ((width, width), BF16),
            (rows, BF16),
        ),
        in_specs=[smem_spec()] * 2 + [vmem_spec()] * 20 + [hbm_spec()],
        out_specs=tuple([vmem_spec()] * 4) + (hbm_spec(),),
        scratch_shapes=[
            pltpu.SemaphoreType.DMA,
            pltpu.VMEM((TILE, width), F32),
            pltpu.VMEM((TILE, width), F32),
            pltpu.VMEM((length, TILE), F32),
            pltpu.VMEM((mem_length, TILE), F32),
            pltpu.VMEM(rows, BF16),
            pltpu.VMEM(rows[::-1], BF16),
            pltpu.VMEM(rows[::-1], BF16),
            pltpu.VMEM((width, both), BF16),
            pltpu.VMEM(rows[::-1], BF16),
            pltpu.VMEM(rows, BF16),
            pltpu.VMEM((both, width), F32),
            pltpu.VMEM((both, width), F32),
            pltpu.VMEM((both, width), BF16),
            pltpu.VMEM((both, width), BF16),
            pltpu.VMEM((width, 2 * QUERY_TILE), BF16),
            pltpu.VMEM((width, 2 * QUERY_TILE), BF16),
            pltpu.VMEM((2 * QUERY_TILE, width), BF16),
            pltpu.VMEM((2 * QUERY_TILE, width), BF16),
            pltpu.VMEM((width, QUERY_TILE), F32),
            pltpu.VMEM((TILE, width), F32),
            pltpu.VMEM((width, TILE), F32),
        ],
        compiler_params=compute_params(),
        name="layer_backward",
    )(
        time_steps, bounds, grad_after, memory[0], dec, mem, weights, small, start, q, k, v,
        after_low, cq, ck, cv, mixed, lse, cross, cross_lse, d_rows, d_hidden,
        layer_part,
    )
    if direct:
        sums, d_ffn = scatter_sums(n, d_attn, d_small, hidden_sums[0])
        *d_weights, d_wide, d_tall, d_table, g1, b1, g2, b2, d_last, d_bias = split_sums(
            sums, d_ffn, steps_count
        )
    else:
        d_expand, d_shrink = hidden_sums
        totals = lax.psum_scatter(
            jnp.concatenate([d_attn, d_expand, d_small[None]]).astype(F32),
            "dp", scatter_dimension=1, tiled=True,
        )
        d_tall = lax.psum_scatter(d_shrink.astype(F32), "dp", scatter_dimension=0, tiled=True)
        d_weights = [totals[j] for j in range(8)]
        d_wide = jnp.concatenate([totals[8 + j] for j in range(hidden // width)], axis=1)
        d_little = totals[-1]
        d_table = d_little[:, :steps_count]
        g1, b1, g2, b2, d_last = (d_little[:, 64 + j] for j in range(5))
        d_bias = d_little[0, TILE : TILE + hidden // n]
    return (
        layer_out[None], tokens_grad[None], memory_grad[None], d_table, g1, b1, *d_weights,
        g2, b2, d_wide, d_bias, d_tall, d_last,
    )


def solution(mesh):
    n = mesh.shape["dp"]
    three, two, one = P("dp", None, None), P("dp", None), P("dp")
    return jax.shard_map(
        functools.partial(per_device, n),
        mesh=mesh,
        in_specs=(three,) * 3 + (two,) * 4 + (one,) * 2 + (two,) * 8 + (one,) * 2
        + (two, one, two, one),
        out_specs=(three,) * 3 + (two,) + (one,) * 2 + (two,) * 8 + (one,) * 2
        + (two, one, two, one),
        check_vma=False,
    )
```
